256 devices in a mesh: lat: 16 (over y, x), lon: 4 (over z_hi, core), ch: 4 (over z_lo).
Axes of the slice: x: 4, y: 4, z: 8 (z_hi: 2, z_lo: 4; z = z_hi * 4 + z_lo), core: 2. Of those that a mesh axis runs over, the one named last changes fastest.
Arguments:
- tokens: bfloat16 [384, 768, 512], P('lat', 'ch', 'lon'), may hold values from -6 to 6
- gain_first: float32 [768], P('ch'), may hold values from 0.25 to 1.75
- mode_first: float32 [8, 18432], P('ch'), may hold values from -0.4375 to 0.4375
- mode_second: float32 [8, 18432], P('ch'), may hold values from -0.4375 to 0.4375
- kept_lat: int32 [288], replicated, may hold values from 0 to 383, as said below
- gain_second: float32 [768], replicated, may hold values from 0.25 to 1.75
- w_up: bfloat16 [768, 3072], P(None, 'ch'), may hold values from -0.21875 to 0.21875
- w_down: bfloat16 [3072, 768], P('ch'), may hold values from -0.109375 to 0.109375
Outputs:
- result: bfloat16 [384, 768, 512], P('lat', 'ch', 'lon')
The draws below stay inside these ranges and needn't reach their ends.
Inputs may be any that keep to these rules, and one draw needn't show every extreme that they name: `kept_lat`: 288 distinct latitude wavenumbers in any order; 0 and 383 are always among them.
All inputs are finite; a program needn't handle non-finite values.
Results may differ from the reference program's by a relative error of at most 0.015.
Values may be sent and summed in bfloat16 or wider, within the bound.
No kernel may reach another device: no remote copies, remote signals or barrier semaphores. Data moves between devices by JAX's collectives and lax.ppermute only.
A program may use at most 128 MiB of HBM per device.

```python
import jax
import jax.numpy as jnp
from jax import lax

C = 768
FF = 3072
NB = 8
BS = 96
W = 512
KW = 256
H = 384
KH = 288


def draw_kept_lat(key, part):
    key = jax.random.fold_in(key, 7)
    inner = jax.random.permutation(key, H - 2).astype(jnp.int32) + 1
    picked = inner[:KH - 2]
    ends = jnp.array([0, H - 1], dtype=jnp.int32)
    joined = jnp.concatenate([ends, picked]).astype(jnp.int32)
    order = jax.random.permutation(jax.random.fold_in(key, 8), KH)
    return joined[order].astype(jnp.int32)


def block_scale(rng, extent, cuts, least, top_value):
    def one(dim, blocks):
        steps = jax.random.uniform(jax.random.fold_in(jax.random.fold_in(rng, 6), dim), (blocks,), jnp.float32, least / len(cuts), top_value / len(cuts))
        return jnp.repeat(jnp.exp(steps), extent[dim] // blocks).reshape((-1,) + (1,) * (len(extent) - dim - 1))

    loudness = one(*cuts[0])
    for cut in cuts[1:]:
        loudness = loudness * one(*cut)
    return loudness


def bell_draw(own_key, shape, scale, reach, split=(), kind=jnp.bfloat16):
    result = jax.random.normal(own_key, shape, jnp.float32) * scale
    if len(split) > 0:
        result = block_scale(own_key, shape, split, -0.22, 0.18) * result
    return jnp.clip(result, min=-reach, max=reach).astype(kind)


def setup_inputs(seed: int = 0) -> dict:
    key_of = jax.random.split(jax.random.key(seed), 9)
    tokens = bell_draw(key_of[0], (H, C, W), 1.0, 6.0, ((0, 16), (1, 4), (2, 4)))
    gain_first = jnp.clip(1.0 + 0.15 * jax.random.normal(key_of[1], (C,), jnp.float32), 0.25, 1.75)
    mode_first = bell_draw(key_of[2], (NB, 2 * BS * BS), (2 * BS) ** -0.5, 0.4375, ((0, 4),), jnp.float32)
    mode_second = bell_draw(key_of[3], (NB, 2 * BS * BS), (2 * BS) ** -0.5, 0.4375, ((0, 4),), jnp.float32)
    kept_lat = draw_kept_lat(jax.random.fold_in(key_of[8], 71), 0)
    gain_second = jnp.clip(1.0 + 0.15 * jax.random.normal(key_of[5], (C,), jnp.float32), 0.25, 1.75)
    w_up = bell_draw(key_of[6], (C, FF), C ** -0.5, 0.21875, ((1, 4),))
    w_down = bell_draw(key_of[7], (FF, C), FF ** -0.5, 0.109375, ((0, 4),))
    return {"tokens": tokens, "gain_first": gain_first, "mode_first": mode_first, "mode_second": mode_second, "kept_lat": kept_lat, "gain_second": gain_second, "w_up": w_up, "w_down": w_down}


SHRINK = 0.01
EPSILON = 1e-05
HIGH = lax.Precision.HIGHEST

def layer_norm(values, gain):
    mean = lax.optimization_barrier(jnp.mean(values, axis=-1, keepdims=True))
    spread = lax.optimization_barrier(jnp.mean((values - mean) * (values - mean), axis=-1, keepdims=True))
    return (values - mean) * lax.rsqrt(spread + EPSILON) * gain

def complex_block(real, imag, weight):
    w_real = weight[:, 0]
    w_imag = weight[:, 1]

    def product(left, right):
        return jnp.einsum('pkbi,bio->pkbo', left, right, precision=HIGH)
    return (product(real, w_real) - product(imag, w_imag), product(real, w_imag) + product(imag, w_real))

def shrink(values):
    return jnp.where(values > SHRINK, values - SHRINK, jnp.where(values < -SHRINK, values + SHRINK, 0.0))

def reference(tokens, gain_first, mode_first, mode_second, kept_lat, gain_second, w_up, w_down):
    values = jnp.transpose(tokens, (0, 2, 1)).astype(jnp.float32)
    normed = layer_norm(values, gain_first).astype(jnp.bfloat16)
    spectrum = jnp.fft.rfft2(normed.astype(jnp.float32), axes=(0, 1), norm='ortho')
    chosen = spectrum[kept_lat][:, :KW]
    shape = (KH, KW, NB, BS)
    real = jnp.real(chosen).reshape(shape)
    imag = jnp.imag(chosen).reshape(shape)
    first_w = mode_first.reshape(NB, 2, BS, BS).astype(jnp.float32)
    second_w = mode_second.reshape(NB, 2, BS, BS).astype(jnp.float32)
    real, imag = complex_block(real, imag, first_w)
    real = jnp.maximum(real, 0.0)
    imag = jnp.maximum(imag, 0.0)
    real, imag = complex_block(real, imag, second_w)
    real = shrink(real).reshape(KH, KW, C)
    imag = shrink(imag).reshape(KH, KW, C)
    full_real = jnp.zeros((H, W // 2 + 1, C), jnp.float32).at[kept_lat, :KW].set(real)
    full_imag = jnp.zeros((H, W // 2 + 1, C), jnp.float32).at[kept_lat, :KW].set(imag)
    field = jnp.fft.irfft2(lax.complex(full_real, full_imag), s=(H, W), axes=(0, 1), norm='ortho')
    field = field.astype(jnp.bfloat16)
    first = (values + normed.astype(jnp.float32) + field.astype(jnp.float32)).astype(jnp.bfloat16)

    def one_row(row):
        ready = layer_norm(row.astype(jnp.float32), gain_second).astype(jnp.bfloat16)
        hidden = jax.nn.gelu(jnp.dot(ready, w_up, preferred_element_type=jnp.float32)).astype(jnp.bfloat16)
        mixed = jnp.dot(hidden, w_down, preferred_element_type=jnp.float32)
        return (row.astype(jnp.float32) + mixed).astype(jnp.bfloat16)
    return jnp.transpose(lax.map(one_row, first), (0, 2, 1))
```

```python
import math

import jax
import jax.numpy as jnp
import numpy as np
from jax import lax
from jax.sharding import Mesh, PartitionSpec as P

BS = 96
KW = 256
SHRINK = 0.01
EPSILON = 1e-05
BF16 = jnp.bfloat16
F32 = jnp.float32


def dot(left, right, dims):
    return lax.dot_general(left, right, (dims, ((), ())), preferred_element_type=F32)


def lon_tables(width, dests):
    k = np.arange(KW)
    angle = 2.0 * np.pi * (k[:, None] * np.arange(width)[None, :] % width) / width
    both = np.stack([np.cos(angle), -np.sin(angle)]) / math.sqrt(width)
    forward = both.reshape(2, dests, KW // dests, width).transpose(1, 0, 2, 3)
    weights = np.where(k == 0, 1.0, 2.0)
    inverse = (both * weights[None, :, None]).reshape(2, dests, KW // dests, width)
    inverse = inverse.transpose(1, 0, 2, 3)
    return forward.reshape(2 * KW, width), inverse.reshape(2 * KW, width)


def lat_tables(kept_lat, height):
    h = np.arange(height)
    angle = 2.0 * np.pi * (h[:, None] * h[None, :] % height) / height
    table = np.stack([np.cos(angle), np.sin(angle)], axis=1) / math.sqrt(height)
    table = jnp.asarray(table.reshape(height, 2 * height), BF16)
    pick = (kept_lat[:, None] == jnp.arange(height)[None, :]).astype(BF16)
    kept = dot(pick, table, ((1,), (0,))).astype(BF16)
    return kept[:, :height], kept[:, height:]


def shrink(values):
    return jnp.where(
        values > SHRINK, values - SHRINK, jnp.where(values < -SHRINK, values + SHRINK, 0.0)
    )


def mode_product(values, weight):
    full = jnp.concatenate(
        [
            jnp.concatenate([weight[0], weight[1]], axis=1),
            jnp.concatenate([-weight[1], weight[0]], axis=1),
        ],
        axis=0,
    ).astype(BF16)
    return dot(values.astype(BF16), full, ((2,), (0,)))


def on_device(tokens, gain_first, mode_first, mode_second, kept_lat, gain_second, w_up, w_down):
    rows, chans, cols = tokens.shape
    lat_n, zh_n, co_n, ch_n = (lax.axis_size(a) for a in ("lat", "zh", "co", "ch"))
    lon_n = zh_n * co_n
    width = cols * lon_n
    height = rows * lat_n
    full = chans * ch_n
    dests = lat_n * co_n
    half = rows // co_n
    trip = half // ch_n
    hidden_n = w_up.shape[1]
    zh, co = lax.axis_index("zh"), lax.axis_index("co")

    piece_n = hidden_n // dests
    piece_at = (co * lat_n + lax.axis_index("lat")) * piece_n
    up_piece = lax.dynamic_slice_in_dim(w_up.T, piece_at, piece_n, axis=0)
    down_piece = lax.dynamic_slice_in_dim(w_down.T, piece_at, piece_n, axis=0)
    weights = jnp.stack([up_piece, down_piece])
    weights = lax.all_gather(weights, "ch")
    weights = lax.all_gather(weights, "lat")
    weights = lax.all_gather(weights, "co")

    values = tokens.astype(F32)
    sums = jnp.stack([jnp.sum(values, axis=1), jnp.sum(values * values, axis=1)])
    sums = lax.all_gather(sums, ("zh", "co", "ch"))
    sums = sums.reshape(lon_n, ch_n, 2, ch_n, co_n, trip, cols).sum(axis=1)
    sums = lax.dynamic_index_in_dim(sums, co, axis=3, keepdims=False)
    sums = sums.reshape(lon_n, 2, half, cols) / full
    mean = sums[:, 0]
    scale = lax.rsqrt(sums[:, 1] - mean * mean + EPSILON)

    parts = tokens.reshape(ch_n, co_n, trip, zh_n, BS, cols).transpose(3, 1, 0, 2, 4, 5)
    parts = parts.reshape(lon_n, half, BS, cols)
    strips = lax.all_to_all(parts, ("zh", "co"), split_axis=0, concat_axis=0, tiled=True)
    gain = lax.dynamic_slice_in_dim(gain_first, zh * BS, BS)
    strips = strips.astype(F32)
    normed = (
        (strips - mean[:, :, None, :]) * scale[:, :, None, :] * gain[None, None, :, None]
    ).astype(BF16)

    forward, inverse = lon_tables(width, dests)
    forward = jnp.asarray(forward, BF16).reshape(2 * KW, lon_n, cols)
    inverse = jnp.asarray(inverse, BF16)
    spec = jnp.einsum("mlw,lrcw->mrc", forward, normed, preferred_element_type=F32)
    spec = spec.astype(BF16).reshape(dests, 2 * KW // dests, half * BS)
    columns = lax.all_to_all(spec, ("lat", "co"), split_axis=0, concat_axis=0, tiled=True)

    modes = KW // dests
    columns = columns.reshape(lat_n, co_n, 2, modes, ch_n, trip, BS)
    columns = columns.transpose(2, 0, 4, 1, 5, 3, 6).reshape(2, height, modes * BS)
    cosine, sine = lat_tables(kept_lat, height)
    left = jnp.concatenate(
        [jnp.concatenate([cosine, sine], axis=1), jnp.concatenate([-sine, cosine], axis=1)], axis=0
    )
    kept = kept_lat.shape[0]
    moved = dot(left, columns.reshape(2 * height, modes * BS), ((1,), (0,)))
    moved = moved.reshape(2, kept, modes, BS).transpose(1, 2, 0, 3).reshape(kept, modes, 2 * BS)
    first_w = lax.dynamic_index_in_dim(mode_first, zh, axis=0, keepdims=False).reshape(2, BS, BS)
    second_w = lax.dynamic_index_in_dim(mode_second, zh, axis=0, keepdims=False).reshape(2, BS, BS)
    inner = jnp.maximum(mode_product(moved, first_w), 0.0)
    outer = shrink(mode_product(inner, second_w)).astype(BF16)
    outer = outer.reshape(kept, modes, 2, BS).transpose(2, 0, 1, 3).reshape(2 * kept, modes * BS)
    back = dot(left, outer, ((0,), (0,))).astype(BF16)
    back = back.reshape(2, lat_n, ch_n, co_n, trip, modes, BS).transpose(1, 3, 0, 5, 2, 4, 6)
    back = back.reshape(dests, 2 * modes, half * BS)
    returned = lax.all_to_all(back, ("lat", "co"), split_axis=0, concat_axis=0, tiled=True)

    returned = returned.reshape(2 * KW, half * BS)
    field = dot(returned, inverse, ((0,), (0,))).astype(BF16)
    field = field.reshape(half, BS, lon_n, cols).transpose(2, 0, 1, 3)
    first = (strips + normed.astype(F32) + field.astype(F32)).astype(BF16)
    first = first.reshape(lon_n, ch_n, trip, BS, cols)
    first = first.reshape(lon_n * ch_n, trip, BS, cols)
    whole = lax.all_to_all(first, ("zh", "co", "ch"), split_axis=0, concat_axis=0, tiled=True)
    whole = whole.reshape(zh_n, co_n, ch_n, trip, BS, cols).transpose(1, 3, 2, 0, 4, 5)
    whole = whole.reshape(co_n * trip, full, cols).astype(F32)

    center = jnp.mean(whole, axis=1, keepdims=True)
    spread = jnp.mean((whole - center) * (whole - center), axis=1, keepdims=True)
    ready = ((whole - center) * lax.rsqrt(spread + EPSILON) * gain_second[None, :, None]).astype(
        BF16
    )
    weights = weights.transpose(3, 2, 0, 1, 4, 5).reshape(2, ch_n, -1, full)
    hidden = jnp.einsum("gfc,rcw->gfrw", weights[0], ready, preferred_element_type=F32)
    hidden = jax.nn.gelu(hidden).astype(BF16)
    mixed = jnp.einsum("gcf,gfrw->rcw", weights[1], hidden, preferred_element_type=F32)
    result = (whole + mixed).astype(BF16)
    result = result.reshape(co_n * trip, ch_n, chans, cols).transpose(1, 0, 2, 3)
    result = lax.all_to_all(result, "ch", split_axis=0, concat_axis=0, tiled=True)
    return result.reshape(rows, chans, cols)


def solution(mesh):
    grid = mesh.devices
    lat_n, lon_n, ch_n = grid.shape
    split = Mesh(grid.reshape(lat_n, 2, lon_n // 2, ch_n), ("lat", "zh", "co", "ch"))
    lon = ("zh", "co")
    return jax.shard_map(
        on_device,
        mesh=split,
        in_specs=(
            P("lat", "ch", lon),
            P("ch"),
            P("ch", None),
            P("ch", None),
            P(),
            P(),
            P(None, "ch"),
            P("ch", None),
        ),
        out_specs=P("lat", "ch", lon),
        check_vma=False,
    )
```

```python
import functools
import math

import jax
import jax.numpy as jnp
import numpy as np
from jax import lax
from jax.experimental import pallas as pl
from jax.experimental.pallas import tpu as pltpu
from jax.sharding import Mesh, PartitionSpec as P

BS = 96
KW = 256
LANES = 128
SHRINK = 0.01
EPSILON = 1e-05
BF16 = jnp.bfloat16
F32 = jnp.float32
VMEM_LIMIT = 40 * 1024 * 1024


def dot(left, right, dims=((1,), (0,))):
    return lax.dot_general(left, right, (dims, ((), ())), preferred_element_type=F32)


def whole(shape):
    return pl.BlockSpec(shape, lambda *_: (0,) * len(shape))


def call(kernel, scalars, args, outs, scratch, flops):
    moved = sum(a.size * a.dtype.itemsize for a in (*args, *outs))
    return pl.pallas_call(
        kernel,
        grid_spec=pltpu.PrefetchScalarGridSpec(
            num_scalar_prefetch=1,
            grid=(1,),
            in_specs=[whole(a.shape) for a in args],
            out_specs=[whole(o.shape) for o in outs],
            scratch_shapes=scratch,
        ),
        out_shape=outs,
        compiler_params=pltpu.CompilerParams(vmem_limit_bytes=VMEM_LIMIT),
        cost_estimate=pl.CostEstimate(flops=flops, bytes_accessed=moved, transcendentals=0),
    )(scalars, *args)


def lon_tables(width, dests):
    k = np.arange(KW)
    angle = 2.0 * np.pi * (k[:, None] * np.arange(width)[None, :] % width) / width
    both = np.stack([np.cos(angle), -np.sin(angle)]) / math.sqrt(width)
    forward = both.reshape(2, dests, KW // dests, width).transpose(1, 0, 2, 3)
    weights = np.where(k == 0, 1.0, 2.0)
    inverse = (both * weights[None, :, None]).reshape(2, dests, KW // dests, width)
    inverse = inverse.transpose(1, 0, 2, 3)
    return forward.reshape(2 * KW, width), inverse.reshape(2 * KW, width)


def lat_table(kept_lat, height, order):
    h = np.arange(height)
    angle = 2.0 * np.pi * (h[:, None] * h[order][None, :] % height) / height
    cosine, sine = np.cos(angle) / math.sqrt(height), np.sin(angle) / math.sqrt(height)
    table = np.concatenate([cosine, sine, -sine, cosine], axis=1)
    pick = (kept_lat[:, None] == jnp.arange(height)[None, :]).astype(BF16)
    kept = dot(pick, jnp.asarray(table, BF16)).astype(BF16)
    return jnp.concatenate([kept[:, : 2 * height], kept[:, 2 * height :]], axis=0)


def mode_weight(flat):
    weight = flat.reshape(2, BS, BS)
    weight = jnp.pad(weight, ((0, 0), (0, LANES - BS), (0, LANES - BS)))
    return jnp.concatenate(
        [
            jnp.concatenate([weight[0], weight[1]], axis=1),
            jnp.concatenate([-weight[1], weight[0]], axis=1),
        ],
        axis=0,
    ).astype(BF16)


def forward_kernel(full, at, own, near, far, across, stats, gain, table, spec, base, normed):
    core, lon = at[0], at[2]
    parts = (
        lambda c, t: own[c, core, t, at[1]],
        lambda c, t: near[c, t],
        lambda c, t: far[c, core, t],
        lambda c, t: across[c, t],
    )
    groups, trip = near.shape[0], near.shape[1]
    for d, part in enumerate(parts):
        lanes = pl.ds(pl.multiple_of((lon ^ d) * LANES, LANES), LANES)
        mean = stats[d, 0] / full
        scale = lax.rsqrt(stats[d, 1] / full - mean * mean + EPSILON)
        for c in range(groups):
            for t in range(trip):
                r = c * trip + t
                values = part(c, t).astype(F32)
                value = (values - mean[r : r + 1]) * scale[r : r + 1] * gain[...]
                value = value.astype(BF16)
                rows = slice(r * BS, (r + 1) * BS)
                normed[rows, lanes] = value
                base[rows, lanes] = values + value.astype(F32)
    result = dot(table[...], normed[...], ((1,), (1,)))
    spec[...] = result.astype(BF16).reshape(spec.shape)


def middle_kernel(at, columns, left, right, first_w, second_w, out, wide, stacked, mid):
    srcs, pairs, inner = columns.shape
    modes = pairs // 2
    local = inner // BS
    height = srcs * local
    kept = left.shape[0] // 2
    tiles = inner // LANES
    for j in range(tiles):
        part = columns[:, :, j * LANES : (j + 1) * LANES]
        wide[j] = part.reshape(srcs * pairs, LANES).astype(F32)
    blank = jnp.zeros((srcs, LANES), F32)
    for t in range(2):
        for k in range(modes):
            take = pl.ds(t * modes + k, srcs, stride=pairs)
            one = jnp.concatenate([wide[j, take, :] for j in range(tiles)] + [blank], axis=1)
            for r in range(local):
                rows = slice(t * height + r * srcs, t * height + (r + 1) * srcs)
                stacked[rows, k * LANES : (k + 1) * LANES] = one[
                    :, r * BS : r * BS + LANES
                ].astype(BF16)
    moved = dot(left[...], stacked[...]).astype(BF16)
    for k in range(modes):
        lanes = slice(k * LANES, (k + 1) * LANES)
        both = jnp.concatenate([moved[:kept, lanes], moved[kept:, lanes]], axis=1)
        both = jnp.maximum(dot(both, first_w[...]), 0.0).astype(BF16)
        both = dot(both, second_w[...])
        both = jnp.where(
            both > SHRINK, both - SHRINK, jnp.where(both < -SHRINK, both + SHRINK, 0.0)
        ).astype(BF16)
        mid[:kept, lanes] = both[:, :LANES]
        mid[kept:, lanes] = both[:, LANES:]
    back = dot(right[...], mid[...])
    for t in range(2):
        for k in range(modes):
            lanes = slice(k * LANES, k * LANES + BS)
            one = jnp.concatenate(
                [
                    back[t * height + r * srcs : t * height + (r + 1) * srcs, lanes]
                    for r in range(local)
                ],
                axis=1,
            )
            for j in range(tiles):
                put = pl.ds(t * modes + k, srcs, stride=pairs)
                wide[j, put, :] = one[:, j * LANES : (j + 1) * LANES]
    for j in range(tiles):
        part = wide[j].astype(BF16).reshape(srcs, pairs, LANES)
        out[:, :, j * LANES : (j + 1) * LANES] = part


def inverse_kernel(at, returned, table, base, *refs):
    outs, first = refs[:-1], refs[-1]
    field = dot(returned[...], table[...], ((0,), (0,))).astype(BF16).astype(F32)
    first[...] = (base[...] + field).astype(BF16)
    count = len(outs)
    cores, trip = outs[0].shape[0], outs[0].shape[1]
    groups = first.shape[0] // (trip * BS)
    for d, out in enumerate(outs):
        place = lax.rem(at[0] + d, count)
        high, low = place // groups, lax.rem(place, groups)
        rows = pl.ds(pl.multiple_of(low * (trip * BS), trip * BS), trip * BS)
        for c in range(cores):
            lanes = pl.ds(pl.multiple_of((high * cores + c) * LANES, LANES), LANES)
            out[c] = first[rows, lanes].reshape(trip, BS, LANES)


def token_kernel(at, *refs):
    mine, theirs, gain, up, down = refs[:8], refs[8], refs[9], refs[10], refs[11]
    outs, (first, ready, total) = refs[12:16], refs[16:]
    step = pl.program_id(0)
    core = at[1]
    trip = theirs.shape[1]
    groups = len(outs)
    count = len(mine)

    @pl.when(step == 0)
    def _():
        for d, ref in enumerate(mine):
            place = lax.rem(at[0] - d + count, count)
            row = (lax.rem(place, groups) * (count // groups) + place // groups) * BS
            rows = pl.ds(pl.multiple_of(row, BS), BS)
            for t in range(trip):
                own = pl.ds(pl.multiple_of((core * trip + t) * LANES, LANES), LANES)
                first[rows, own] = ref[core, t]
                other = pl.ds(pl.multiple_of(((1 - core) * trip + t) * LANES, LANES), LANES)
                first[rows, other] = theirs[d, t]
        values = first[...].astype(F32)
        mean = jnp.mean(values, axis=0, keepdims=True)
        values = values - mean
        spread = jnp.mean(values * values, axis=0, keepdims=True)
        ready[...] = (values * lax.rsqrt(spread + EPSILON) * gain[...]).astype(BF16)
        total[...] = first[...].astype(F32)

    side = first.shape[0]
    hidden = dot(up[...].reshape(-1, side), ready[...])
    hidden = jax.nn.gelu(hidden).astype(BF16)
    total[...] += dot(down[...].reshape(side, -1), hidden)

    @pl.when(step == pl.num_programs(0) - 1)
    def _():
        chans = outs[0].shape[1]
        for d, out in enumerate(outs):
            low = lax.rem(lax.rem(at[0], groups) + d, groups)
            rows = pl.ds(pl.multiple_of(low * chans, chans), chans)
            for r in range(out.shape[0]):
                out[r] = total[rows, r * LANES : (r + 1) * LANES].astype(BF16)


def on_device(tokens, gain_first, mode_first, mode_second, kept_lat, gain_second, w_up, w_down):
    rows, chans, cols = tokens.shape
    lat_n, zh_n, co_n, ch_n = (lax.axis_size(a) for a in ("lat", "zh", "co", "ch"))
    lon_n, z_n = zh_n * co_n, zh_n * ch_n
    width = cols * lon_n
    height = rows * lat_n
    full = chans * ch_n
    dests = lat_n * co_n
    half = rows // co_n
    trip = half // ch_n
    lat, zh, co, ch = (lax.axis_index(a) for a in ("lat", "zh", "co", "ch"))
    lon = zh * co_n + co
    z = zh * ch_n + ch
    swap = [(0, 1), (1, 0)]

    def ring(array, axes, count, step):
        return lax.ppermute(array, axes, [(i, (i + step) % count) for i in range(count)])

    values = tokens.astype(F32)
    sums = jnp.stack([jnp.sum(values, axis=1), jnp.sum(values * values, axis=1)])
    sums = sums + sum(ring(sums, "ch", ch_n, d) for d in range(1, ch_n))
    shared = [sums] + [
        lax.ppermute(sums, ("zh", "co"), [(i, i ^ d) for i in range(lon_n)])
        for d in range(1, lon_n)
    ]
    stats = jnp.stack(shared).reshape(lon_n, 2, ch_n, co_n, trip, cols)
    stats = lax.dynamic_index_in_dim(stats, co, axis=3, keepdims=False)
    stats = stats.reshape(lon_n, 2, half, cols)

    own = tokens.reshape(ch_n, co_n, trip, zh_n, BS, cols)
    far = lax.ppermute(
        lax.dynamic_index_in_dim(own, 1 - zh, axis=3, keepdims=False), "zh", swap
    )
    near = lax.dynamic_index_in_dim(own, zh, axis=3, keepdims=False)
    near = lax.dynamic_index_in_dim(near, 1 - co, axis=1, keepdims=False)
    near = lax.ppermute(near, "co", swap)
    across = lax.dynamic_index_in_dim(far, 1 - co, axis=1, keepdims=False)
    across = lax.ppermute(across, "co", swap)

    picked = jnp.where(co == 0, w_up, w_down).T
    piece_n = picked.shape[0] // lat_n
    piece = lax.dynamic_slice_in_dim(picked, lat * piece_n, piece_n, axis=0)
    pieces = jnp.stack([piece] + [ring(piece, "ch", ch_n, d) for d in range(1, ch_n)])
    weights = lax.all_gather(pieces, ("lat", "co"))
    weights = weights.reshape(lat_n, co_n, ch_n, piece_n, full)

    forward, inverse = lon_tables(width, dests)
    gain = lax.dynamic_slice_in_dim(gain_first, zh * BS, BS)
    gain = jnp.broadcast_to(gain[:, None], (BS, cols))
    at = jnp.stack([co, zh, lon]).astype(jnp.int32)
    wide_n = half * BS
    spec, base = call(
        functools.partial(forward_kernel, float(full)),
        at,
        (own, near, far, across, stats, gain, jnp.asarray(forward, BF16)),
        (
            jax.ShapeDtypeStruct((dests, 2 * KW // dests, wide_n), BF16),
            jax.ShapeDtypeStruct((wide_n, width), F32),
        ),
        [pltpu.VMEM((wide_n, width), BF16)],
        4 * KW * width * wide_n,
    )
    columns = lax.all_to_all(spec, ("lat", "co"), split_axis=0, concat_axis=0, tiled=True)

    modes = KW // dests
    order = np.arange(height).reshape(lat_n, ch_n, co_n, trip).transpose(1, 3, 0, 2).reshape(-1)
    left = lat_table(kept_lat, height, order)
    kept = kept_lat.shape[0]
    first_w = mode_weight(lax.dynamic_index_in_dim(mode_first, zh, axis=0, keepdims=False))
    second_w = mode_weight(lax.dynamic_index_in_dim(mode_second, zh, axis=0, keepdims=False))
    (back,) = call(
        middle_kernel,
        at,
        (columns, left, left.T, first_w, second_w),
        (jax.ShapeDtypeStruct(columns.shape, BF16),),
        [
            pltpu.VMEM((wide_n // LANES, dests * 2 * modes, LANES), F32),
            pltpu.VMEM((2 * height, modes * LANES), BF16),
            pltpu.VMEM((2 * kept, modes * LANES), BF16),
        ],
        16 * height * kept * modes * LANES,
    )
    returned = lax.all_to_all(back, ("lat", "co"), split_axis=0, concat_axis=0, tiled=True)

    at = jnp.stack([z, co]).astype(jnp.int32)
    firsts = call(
        inverse_kernel,
        at,
        (returned.reshape(2 * KW, wide_n), jnp.asarray(inverse, BF16), base),
        tuple(jax.ShapeDtypeStruct((co_n, trip, BS, cols), BF16) for _ in range(z_n)),
        [pltpu.VMEM((wide_n, width), BF16)],
        4 * KW * width * wide_n,
    )
    mine = [firsts[0]] + [ring(firsts[d], ("zh", "ch"), z_n, d) for d in range(1, z_n)]
    theirs = jnp.stack(
        [lax.dynamic_index_in_dim(m, 1 - co, axis=0, keepdims=False) for m in mine]
    )
    theirs = lax.ppermute(theirs, "co", swap)

    tokens_n = co_n * trip * cols
    gain = jnp.broadcast_to(gain_second[:, None], (full, tokens_n))
    once = [whole(m.shape) for m in mine] + [whole(theirs.shape), whole(gain.shape)]
    weight_block = (lat_n, None, None, piece_n, full)
    results = pl.pallas_call(
        token_kernel,
        grid_spec=pltpu.PrefetchScalarGridSpec(
            num_scalar_prefetch=1,
            grid=(ch_n,),
            in_specs=once
            + [
                pl.BlockSpec(weight_block, lambda i, at: (0, 0, i, 0, 0)),
                pl.BlockSpec(weight_block, lambda i, at: (0, 1, i, 0, 0)),
            ],
            out_specs=[whole((co_n * trip, chans, cols))] * ch_n,
            scratch_shapes=[
                pltpu.VMEM((full, tokens_n), BF16),
                pltpu.VMEM((full, tokens_n), BF16),
                pltpu.VMEM((full, tokens_n), F32),
            ],
        ),
        out_shape=[jax.ShapeDtypeStruct((co_n * trip, chans, cols), BF16)] * ch_n,
        compiler_params=pltpu.CompilerParams(vmem_limit_bytes=VMEM_LIMIT),
        cost_estimate=pl.CostEstimate(
            flops=4 * full * full * ch_n * tokens_n,
            bytes_accessed=weights.size * 2,
            transcendentals=full * ch_n * tokens_n,
        ),
    )(at, *mine, theirs, gain, weights, weights)
    output = jnp.zeros((ch_n, co_n * trip, chans, cols), BF16)
    for d, piece in enumerate(results):
        piece = piece if d == 0 else ring(piece, "ch", ch_n, d)
        output = lax.dynamic_update_index_in_dim(output, piece, lax.rem(ch - d + ch_n, ch_n), 0)
    return output.reshape(rows, chans, cols)


def solution(mesh):
    grid = mesh.devices
    lat_n, lon_n, ch_n = grid.shape
    split = Mesh(grid.reshape(lat_n, 2, lon_n // 2, ch_n), ("lat", "zh", "co", "ch"))
    lon = ("zh", "co")
    return jax.shard_map(
        on_device,
        mesh=split,
        in_specs=(
            P("lat", "ch", lon),
            P("ch"),
            P("ch", None),
            P("ch", None),
            P(),
            P(),
            P(None, "ch"),
            P("ch", None),
        ),
        out_specs=P("lat", "ch", lon),
        check_vma=False,
    )
```

```python
import functools
import math

import jax
import jax.numpy as jnp
import numpy as np
from jax import lax
from jax.experimental import pallas as pl
from jax.experimental.pallas import tpu as pltpu
from jax.sharding import Mesh, PartitionSpec as P

BS = 96
KW = 256
LANES = 128
SHRINK = 0.01
EPSILON = 1e-05
BF16 = jnp.bfloat16
F32 = jnp.float32
SMALL = 32 * 1024 * 1024
LARGE = 56 * 1024 * 1024


def dot(left, right, dims=((1,), (0,))):
    return lax.dot_general(left, right, (dims, ((), ())), preferred_element_type=F32)


def whole(shape):
    return pl.BlockSpec(shape, lambda *_: (0,) * len(shape))


def call(kernel, scalars, args, outs, scratch, flops, limit=SMALL):
    moved = sum(a.size * a.dtype.itemsize for a in (*args, *outs))
    return pl.pallas_call(
        kernel,
        grid_spec=pltpu.PrefetchScalarGridSpec(
            num_scalar_prefetch=1,
            grid=(1,),
            in_specs=[whole(a.shape) for a in args],
            out_specs=[whole(o.shape) for o in outs],
            scratch_shapes=scratch,
        ),
        out_shape=outs,
        compiler_params=pltpu.CompilerParams(vmem_limit_bytes=limit),
        cost_estimate=pl.CostEstimate(flops=flops, bytes_accessed=moved, transcendentals=0),
    )(scalars, *args)


def lon_tables(width, dests):
    k = np.arange(KW)
    angle = 2.0 * np.pi * (k[:, None] * np.arange(width)[None, :] % width) / width
    both = np.stack([np.cos(angle), -np.sin(angle)]) / math.sqrt(width)
    forward = both.reshape(2, dests, KW // dests, width).transpose(1, 0, 2, 3)
    weights = np.where(k == 0, 1.0, 2.0)
    inverse = (both * weights[None, :, None]).reshape(2, dests, KW // dests, width)
    inverse = inverse.transpose(1, 0, 2, 3)
    return forward.reshape(2 * KW, width), inverse.reshape(2 * KW, width)


def lat_table(kept_lat, height, order):
    h = np.arange(height)
    angle = 2.0 * np.pi * (h[:, None] * h[order][None, :] % height) / height
    cosine, sine = np.cos(angle) / math.sqrt(height), np.sin(angle) / math.sqrt(height)
    table = np.concatenate([cosine, sine, -sine, cosine], axis=1)
    pick = (kept_lat[:, None] == jnp.arange(height)[None, :]).astype(BF16)
    kept = dot(pick, jnp.asarray(table, BF16)).astype(BF16)
    return jnp.concatenate([kept[:, : 2 * height], kept[:, 2 * height :]], axis=0)


def mode_weight(flat):
    weight = flat.reshape(2, BS, BS)
    weight = jnp.pad(weight, ((0, 0), (0, LANES - BS), (0, LANES - BS)))
    return jnp.concatenate(
        [
            jnp.concatenate([weight[0], weight[1]], axis=1),
            jnp.concatenate([-weight[1], weight[0]], axis=1),
        ],
        axis=0,
    ).astype(BF16)


def strips(at, own, near, far, across):
    core, high, lon = at[0], at[1], at[2]
    trip = near.shape[1]
    parts = (
        lambda c, t: own[c, core, t, high],
        lambda c, t: near[c, t],
        lambda c, t: far[c, core, t],
        lambda c, t: across[c, t],
    )
    for d, part in enumerate(parts):
        lanes = pl.ds(pl.multiple_of((lon ^ d) * LANES, LANES), LANES)
        for r in range(near.shape[0] * trip):
            yield r, lanes, part(r // trip, r % trip).astype(F32)


def forward_kernel(full, at, own, near, far, across, chip, partner, gain, table, *refs):
    spec, base, normed, mean, scale = refs
    for d in range(4):
        stats = (chip if d < 2 else partner)[d % 2] / full
        mean[d] = stats[0]
        scale[d] = lax.rsqrt(stats[1] - stats[0] * stats[0] + EPSILON)
    count, trip = near.shape[0] * near.shape[1], near.shape[1]
    for i, (r, lanes, values) in enumerate(strips(at, own, near, far, across)):
        d = i // count
        low = r + (r // trip) * trip
        picked = []
        for ref in (mean, scale):
            rows = ref[d, low : low + 1], ref[d, low + trip : low + trip + 1]
            picked.append(jnp.where(at[0] == 0, *rows))
        value = ((values - picked[0]) * picked[1] * gain[...]).astype(BF16)
        rows = slice(r * BS, (r + 1) * BS)
        normed[rows, lanes] = value
        base[rows, lanes] = values + value.astype(F32)
    result = dot(table[...], normed[...], ((1,), (1,)))
    spec[...] = result.astype(BF16).reshape(spec.shape)


def middle_kernel(at, columns, left, first_w, second_w, out, wide, stacked, mid):
    srcs, pairs, inner = columns.shape
    modes = pairs // 2
    local = inner // BS
    height = srcs * local
    kept = left.shape[0] // 2
    tiles = inner // LANES
    for j in range(tiles):
        part = columns[:, :, j * LANES : (j + 1) * LANES]
        wide[j] = part.reshape(srcs * pairs, LANES).astype(F32)
    blank = jnp.zeros((srcs, LANES), F32)
    for t in range(2):
        for k in range(modes):
            take = pl.ds(t * modes + k, srcs, stride=pairs)
            one = jnp.concatenate([wide[j, take, :] for j in range(tiles)] + [blank], axis=1)
            for r in range(local):
                rows = slice(t * height + r * srcs, t * height + (r + 1) * srcs)
                stacked[rows, k * LANES : (k + 1) * LANES] = one[
                    :, r * BS : r * BS + LANES
                ].astype(BF16)
    moved = dot(left[...], stacked[...]).astype(BF16)
    for k in range(modes):
        lanes = slice(k * LANES, (k + 1) * LANES)
        both = jnp.concatenate([moved[:kept, lanes], moved[kept:, lanes]], axis=1)
        both = jnp.maximum(dot(both, first_w[...]), 0.0).astype(BF16)
        both = dot(both, second_w[...])
        both = jnp.where(
            both > SHRINK, both - SHRINK, jnp.where(both < -SHRINK, both + SHRINK, 0.0)
        ).astype(BF16)
        mid[:kept, lanes] = both[:, :LANES]
        mid[kept:, lanes] = both[:, LANES:]
    back = dot(left[...], mid[...], ((0,), (0,)))
    for t in range(2):
        for k in range(modes):
            lanes = slice(k * LANES, k * LANES + BS)
            one = jnp.concatenate(
                [
                    back[t * height + r * srcs : t * height + (r + 1) * srcs, lanes]
                    for r in range(local)
                ],
                axis=1,
            )
            for j in range(tiles):
                put = pl.ds(t * modes + k, srcs, stride=pairs)
                wide[j, put, :] = one[:, j * LANES : (j + 1) * LANES]
    for j in range(tiles):
        part = wide[j].astype(BF16).reshape(srcs, pairs, LANES)
        out[:, :, j * LANES : (j + 1) * LANES] = part


def inverse_kernel(at, returned, table, base, *refs):
    outs, first = refs[:-1], refs[-1]
    field = dot(returned[...], table[...], ((0,), (0,))).astype(BF16).astype(F32)
    first[...] = (base[...] + field).astype(BF16)
    count = len(outs)
    cores, trip = outs[0].shape[0], outs[0].shape[1]
    groups = first.shape[0] // (trip * BS)
    for d, out in enumerate(outs):
        place = lax.rem(at[0] + d, count)
        high, low = place // groups, lax.rem(place, groups)
        rows = pl.ds(pl.multiple_of(low * (trip * BS), trip * BS), trip * BS)
        for c in range(cores):
            lanes = pl.ds(pl.multiple_of((high * cores + c) * LANES, LANES), LANES)
            out[c] = first[rows, lanes].reshape(trip, BS, LANES)


def token_kernel(order, at, *refs):
    count = len(order)
    mine, theirs, gain, weights = refs[:count], *refs[count : count + 3]
    outs, (first, ready, total, held, done) = refs[count + 3 : -5], refs[-5:]
    core = at[1]
    trip = theirs.shape[1]
    groups = len(outs)
    steps = held.shape[0]
    pair = weights.shape[2]
    copies = [
        pltpu.make_async_copy(weights.at[:, i // pair, i % pair], held.at[i], done.at[i])
        for i in range(steps)
    ]
    for copy in copies:
        copy.start()
    for i, ref in enumerate(mine):
        place = lax.rem(at[0] - order[i] + count, count)
        row = (lax.rem(place, groups) * (count // groups) + place // groups) * BS
        rows = pl.ds(pl.multiple_of(row, BS), BS)
        for t in range(trip):
            own = pl.ds(pl.multiple_of((core * trip + t) * LANES, LANES), LANES)
            first[rows, own] = ref[core, t]
            other = pl.ds(pl.multiple_of(((1 - core) * trip + t) * LANES, LANES), LANES)
            first[rows, other] = theirs[i, t]
    for r in range(2 * trip):
        lanes = slice(r * LANES, (r + 1) * LANES)
        values = first[:, lanes].astype(F32)
        total[:, lanes] = values
        values = values - jnp.mean(values, axis=0, keepdims=True)
        spread = jnp.mean(values * values, axis=0, keepdims=True)
        ready[:, lanes] = (values * lax.rsqrt(spread + EPSILON) * gain[...]).astype(BF16)
    side = first.shape[0]
    for i, copy in enumerate(copies):
        copy.wait()
        hidden = dot(held[i, :, 0].reshape(-1, side), ready[...])
        hidden = jax.nn.gelu(hidden).astype(BF16)
        total[...] += dot(held[i, :, 1].reshape(side, -1), hidden)
    chans = outs[0].shape[1]
    for d, out in enumerate(outs):
        low = lax.rem(lax.rem(at[0], groups) + d, groups)
        rows = pl.ds(pl.multiple_of(low * chans, chans), chans)
        for r in range(out.shape[0]):
            out[r] = total[rows, r * LANES : (r + 1) * LANES].astype(BF16)


def on_device(tokens, gain_first, mode_first, mode_second, kept_lat, gain_second, w_up, w_down):
    rows, chans, cols = tokens.shape
    lat_n, zh_n, co_n, ch_n = (lax.axis_size(a) for a in ("lat", "zh", "co", "ch"))
    lon_n, z_n = zh_n * co_n, zh_n * ch_n
    width = cols * lon_n
    height = rows * lat_n
    full = chans * ch_n
    dests = lat_n * co_n
    half = rows // co_n
    trip = half // ch_n
    lat, zh, co, ch = (lax.axis_index(a) for a in ("lat", "zh", "co", "ch"))
    lon = zh * co_n + co
    z = zh * ch_n + ch
    swap = [(0, 1), (1, 0)]

    def ring(array, axes, count, step):
        return lax.ppermute(array, axes, [(i, (i + step) % count) for i in range(count)])

    piece_n = w_up.shape[1] // lat_n
    piece = jnp.stack(
        [
            lax.dynamic_slice_in_dim(w, lat * piece_n, piece_n, axis=1).T
            for w in (w_up, w_down)
        ]
    )
    pieces = [
        lax.ppermute(
            piece,
            ("co", "ch"),
            [(c * ch_n + i, c * ch_n + (i + 2 * c + d) % ch_n) for c in range(co_n) for i in range(ch_n)],
        )
        for d in range(ch_n // co_n)
    ]
    pieces = jnp.stack(pieces)

    values = tokens.astype(F32)
    sums = jnp.stack([jnp.sum(values, axis=1), jnp.sum(values * values, axis=1)])
    sums = sums + sum(ring(sums, "ch", ch_n, d) for d in range(1, ch_n))

    block_gain = lax.dynamic_slice_in_dim(gain_first, zh * BS, BS)
    block_gain = jnp.broadcast_to(block_gain[:, None], (BS, cols))
    second_gain = jnp.broadcast_to(gain_second[:, None], (full, cols))
    place = jnp.stack([co, zh, lon]).astype(jnp.int32)
    column = jnp.stack([z, co]).astype(jnp.int32)
    pieces, sums, sent, block_gain, second_gain, place, column = lax.optimization_barrier(
        (pieces, sums, tokens, block_gain, second_gain, place, column)
    )
    weights = lax.all_gather(pieces, ("lat", "co"))
    own = sent.reshape(ch_n, co_n, trip, zh_n, BS, cols)
    far = lax.ppermute(
        lax.dynamic_index_in_dim(own, 1 - zh, axis=3, keepdims=False), "zh", swap
    )
    chip_sums = jnp.stack([sums, lax.ppermute(sums, "co", swap)])
    partner_sums = lax.ppermute(chip_sums, "zh", swap)
    order = np.arange(height).reshape(lat_n, ch_n, co_n, trip).transpose(1, 3, 0, 2).reshape(-1)
    left = lat_table(kept_lat, height, order)
    kept = kept_lat.shape[0]
    first_w = mode_weight(lax.dynamic_index_in_dim(mode_first, zh, axis=0, keepdims=False))
    second_w = mode_weight(lax.dynamic_index_in_dim(mode_second, zh, axis=0, keepdims=False))
    (far, chip_sums, partner_sums), tables = lax.optimization_barrier(
        (
            (far, chip_sums, partner_sums),
            (left, first_w, second_w),
        )
    )
    left, first_w, second_w = tables
    near = lax.dynamic_index_in_dim(own, zh, axis=3, keepdims=False)
    near = lax.dynamic_index_in_dim(near, 1 - co, axis=1, keepdims=False)
    near = lax.ppermute(near, "co", swap)
    across = lax.dynamic_index_in_dim(far, 1 - co, axis=1, keepdims=False)
    across = lax.ppermute(across, "co", swap)
    forward, inverse = lon_tables(width, dests)
    wide_n = half * BS
    spec, base = call(
        functools.partial(forward_kernel, float(full)),
        place,
        (own, near, far, across, chip_sums, partner_sums, block_gain, jnp.asarray(forward, BF16)),
        (
            jax.ShapeDtypeStruct((dests, 2 * KW // dests, wide_n), BF16),
            jax.ShapeDtypeStruct((wide_n, width), F32),
        ),
        [
            pltpu.VMEM((wide_n, width), BF16),
            pltpu.VMEM((lon_n, rows, cols), F32),
            pltpu.VMEM((lon_n, rows, cols), F32),
        ],
        4 * KW * width * wide_n,
    )
    columns = lax.all_to_all(spec, ("lat", "co"), split_axis=0, concat_axis=0, tiled=True)

    modes = KW // dests
    (back,) = call(
        middle_kernel,
        place,
        (columns, left, first_w, second_w),
        (jax.ShapeDtypeStruct(columns.shape, BF16),),
        [
            pltpu.VMEM((wide_n // LANES, dests * 2 * modes, LANES), F32),
            pltpu.VMEM((2 * height, modes * LANES), BF16),
            pltpu.VMEM((2 * kept, modes * LANES), BF16),
        ],
        16 * height * kept * modes * LANES,
    )
    returned = lax.all_to_all(back, ("lat", "co"), split_axis=0, concat_axis=0, tiled=True)

    returned, weights = lax.optimization_barrier((returned, weights))
    weights = weights.reshape(lat_n, co_n, ch_n // co_n, 2, piece_n, full)
    firsts = call(
        inverse_kernel,
        column,
        (returned.reshape(2 * KW, wide_n), jnp.asarray(inverse, BF16), base),
        tuple(jax.ShapeDtypeStruct((co_n, trip, BS, cols), BF16) for _ in range(z_n)),
        [pltpu.VMEM((wide_n, width), BF16)],
        4 * KW * width * wide_n,
        SMALL,
    )
    order = sorted(range(z_n), key=lambda d: (min(d, z_n - d), -d))
    mine = [ring(firsts[d], ("zh", "ch"), z_n, d) if d else firsts[0] for d in order]
    theirs = jnp.stack(
        [lax.dynamic_index_in_dim(m, 1 - co, axis=0, keepdims=False) for m in mine]
    )
    theirs = lax.ppermute(theirs, "co", swap)

    tokens_n = co_n * trip * cols
    once = [*mine, theirs, second_gain]
    results = pl.pallas_call(
        functools.partial(token_kernel, order),
        grid_spec=pltpu.PrefetchScalarGridSpec(
            num_scalar_prefetch=1,
            grid=(1,),
            in_specs=[whole(a.shape) for a in once] + [pl.BlockSpec(memory_space=pltpu.HBM)],
            out_specs=[whole((co_n * trip, chans, cols))] * ch_n,
            scratch_shapes=[
                pltpu.VMEM((full, tokens_n), BF16),
                pltpu.VMEM((full, tokens_n), BF16),
                pltpu.VMEM((full, tokens_n), F32),
                pltpu.VMEM((ch_n, lat_n, 2, piece_n, full), BF16),
                pltpu.SemaphoreType.DMA((ch_n,)),
            ],
        ),
        out_shape=[jax.ShapeDtypeStruct((co_n * trip, chans, cols), BF16)] * ch_n,
        compiler_params=pltpu.CompilerParams(vmem_limit_bytes=LARGE),
        cost_estimate=pl.CostEstimate(
            flops=4 * full * full * ch_n * tokens_n,
            bytes_accessed=weights.size * 2,
            transcendentals=full * ch_n * tokens_n,
        ),
    )(column, *once, weights)
    output = jnp.zeros((ch_n, co_n * trip, chans, cols), BF16)
    for d, piece in enumerate(results):
        piece = piece if d == 0 else ring(piece, "ch", ch_n, d)
        output = lax.dynamic_update_index_in_dim(output, piece, lax.rem(ch - d + ch_n, ch_n), 0)
    return output.reshape(rows, chans, cols)


def solution(mesh):
    grid = mesh.devices
    lat_n, lon_n, ch_n = grid.shape
    split = Mesh(grid.reshape(lat_n, 2, lon_n // 2, ch_n), ("lat", "zh", "co", "ch"))
    lon = ("zh", "co")
    return jax.shard_map(
        on_device,
        mesh=split,
        in_specs=(
            P("lat", "ch", lon),
            P("ch"),
            P("ch", None),
            P("ch", None),
            P(),
            P(),
            P(None, "ch"),
            P("ch", None),
        ),
        out_specs=P("lat", "ch", lon),
        check_vma=False,
    )
```

```python
import functools
import math

import jax
import jax.numpy as jnp
import numpy as np
from jax import lax
from jax.experimental import pallas as pl
from jax.experimental.pallas import tpu as pltpu
from jax.sharding import Mesh, PartitionSpec as P

BS = 96
KW = 256
LANES = 128
SHRINK = 0.01
EPSILON = 1e-05
BF16 = jnp.bfloat16
F32 = jnp.float32
SMALL = 32 * 1024 * 1024
LARGE = 56 * 1024 * 1024


def dot(left, right, dims=((1,), (0,))):
    return lax.dot_general(left, right, (dims, ((), ())), preferred_element_type=F32)


def whole(shape):
    return pl.BlockSpec(shape, lambda *_: (0,) * len(shape))


def call(kernel, scalars, args, outs, scratch, flops, limit=SMALL):
    moved = sum(a.size * a.dtype.itemsize for a in (*args, *outs))
    return pl.pallas_call(
        kernel,
        grid_spec=pltpu.PrefetchScalarGridSpec(
            num_scalar_prefetch=1,
            grid=(1,),
            in_specs=[whole(a.shape) for a in args],
            out_specs=[whole(o.shape) for o in outs],
            scratch_shapes=scratch,
        ),
        out_shape=outs,
        compiler_params=pltpu.CompilerParams(vmem_limit_bytes=limit),
        cost_estimate=pl.CostEstimate(flops=flops, bytes_accessed=moved, transcendentals=0),
    )(scalars, *args)


def lon_tables(width, dests):
    k = np.arange(KW)
    angle = 2.0 * np.pi * (k[:, None] * np.arange(width)[None, :] % width) / width
    both = np.stack([np.cos(angle), -np.sin(angle)]) / math.sqrt(width)
    forward = both.reshape(2, dests, KW // dests, width).transpose(1, 0, 2, 3)
    weights = np.where(k == 0, 1.0, 2.0)
    inverse = (both * weights[None, :, None]).reshape(2, dests, KW // dests, width)
    inverse = inverse.transpose(1, 0, 2, 3)
    return forward.reshape(2 * KW, width), inverse.reshape(2 * KW, width)


def lat_table(kept_lat, height, order):
    h = np.arange(height)
    angle = 2.0 * np.pi * (h[:, None] * h[order][None, :] % height) / height
    cosine, sine = np.cos(angle) / math.sqrt(height), np.sin(angle) / math.sqrt(height)
    table = np.concatenate([cosine, sine, -sine, cosine], axis=1)
    pick = (kept_lat[:, None] == jnp.arange(height)[None, :]).astype(BF16)
    kept = dot(pick, jnp.asarray(table, BF16)).astype(BF16)
    return jnp.concatenate([kept[:, : 2 * height], kept[:, 2 * height :]], axis=0)


def mode_weight(flat):
    weight = flat.reshape(2, BS, BS)
    weight = jnp.pad(weight, ((0, 0), (0, LANES - BS), (0, LANES - BS)))
    return jnp.concatenate(
        [
            jnp.concatenate([weight[0], weight[1]], axis=1),
            jnp.concatenate([-weight[1], weight[0]], axis=1),
        ],
        axis=0,
    ).astype(BF16)


def forward_kernel(full, start, at, own, near, far, across, chip, partner, gain, table, *refs):
    spec, base, normed, mean, scale = refs
    for d in range(4):
        stats = (chip if d < 2 else partner)[d % 2] / full
        mean[d] = stats[0]
        scale[d] = lax.rsqrt(stats[1] - stats[0] * stats[0] + EPSILON)
    core, high, lon = at[0], at[1], at[2]
    trip, count = own.shape[2], near.shape[1]
    parts = (
        lambda c, t: own[c, core, start + t, high],
        lambda c, t: near[c, t],
        lambda c, t: far[c, core, t],
        lambda c, t: across[c, t],
    )
    for d, part in enumerate(parts):
        lanes = pl.ds(pl.multiple_of((lon ^ d) * LANES, LANES), LANES)
        for c in range(near.shape[0]):
            for t in range(count):
                low = 2 * c * trip + start + t
                picked = []
                for ref in (mean, scale):
                    rows = ref[d, low : low + 1], ref[d, low + trip : low + trip + 1]
                    picked.append(jnp.where(core == 0, *rows))
                values = part(c, t).astype(F32)
                value = ((values - picked[0]) * picked[1] * gain[...]).astype(BF16)
                rows = slice((c * count + t) * BS, (c * count + t + 1) * BS)
                normed[rows, lanes] = value
                base[rows, lanes] = values + value.astype(F32)
    result = dot(table[...], normed[...], ((1,), (1,)))
    spec[...] = result.astype(BF16).reshape(spec.shape)


def middle_kernel(parts, at, *refs):
    columns, (left, first_w, second_w) = refs[:parts], refs[parts : parts + 3]
    out, wide, stacked, mid = refs[parts + 3 :]
    srcs, pairs, inner = out.shape
    modes = pairs // 2
    local = inner // BS
    height = srcs * local
    kept = left.shape[0] // 2
    tiles = inner // LANES
    j = 0
    for column in columns:
        for k in range(column.shape[2] // LANES):
            part = column[:, :, k * LANES : (k + 1) * LANES]
            wide[j] = part.reshape(srcs * pairs, LANES).astype(F32)
            j += 1
    blank = jnp.zeros((srcs, LANES), F32)
    for t in range(2):
        for k in range(modes):
            take = pl.ds(t * modes + k, srcs, stride=pairs)
            one = jnp.concatenate([wide[j, take, :] for j in range(tiles)] + [blank], axis=1)
            for r in range(local):
                rows = slice(t * height + r * srcs, t * height + (r + 1) * srcs)
                stacked[rows, k * LANES : (k + 1) * LANES] = one[
                    :, r * BS : r * BS + LANES
                ].astype(BF16)
    moved = dot(left[...], stacked[...]).astype(BF16)
    for k in range(modes):
        lanes = slice(k * LANES, (k + 1) * LANES)
        both = jnp.concatenate([moved[:kept, lanes], moved[kept:, lanes]], axis=1)
        both = jnp.maximum(dot(both, first_w[...]), 0.0).astype(BF16)
        both = dot(both, second_w[...])
        both = jnp.where(
            both > SHRINK, both - SHRINK, jnp.where(both < -SHRINK, both + SHRINK, 0.0)
        ).astype(BF16)
        mid[:kept, lanes] = both[:, :LANES]
        mid[kept:, lanes] = both[:, LANES:]
    back = dot(left[...], mid[...], ((0,), (0,)))
    for t in range(2):
        for k in range(modes):
            lanes = slice(k * LANES, k * LANES + BS)
            one = jnp.concatenate(
                [
                    back[t * height + r * srcs : t * height + (r + 1) * srcs, lanes]
                    for r in range(local)
                ],
                axis=1,
            )
            for j in range(tiles):
                put = pl.ds(t * modes + k, srcs, stride=pairs)
                wide[j, put, :] = one[:, j * LANES : (j + 1) * LANES]
    for j in range(tiles):
        part = wide[j].astype(BF16).reshape(srcs, pairs, LANES)
        out[:, :, j * LANES : (j + 1) * LANES] = part


def inverse_kernel(chunks, at, returned, table, *refs):
    bases, outs, first = refs[: len(chunks)], refs[len(chunks) : -1], refs[-1]
    field = dot(returned[...], table[...], ((0,), (0,))).astype(BF16).astype(F32)
    ahead = 0
    for base in bases:
        size = base.shape[0]
        first[ahead : ahead + size] = (base[...] + field[ahead : ahead + size]).astype(BF16)
        ahead += size
    count = len(outs)
    cores, trip = outs[0].shape[0], outs[0].shape[1]
    groups = first.shape[0] // (trip * BS)
    for d, out in enumerate(outs):
        place = lax.rem(at[0] + d, count)
        high, low = place // groups, lax.rem(place, groups)
        for start, many in chunks:
            row = start * groups * BS + low * (many * BS)
            rows = pl.ds(pl.multiple_of(row, BS), many * BS)
            for c in range(cores):
                lanes = pl.ds(pl.multiple_of((high * cores + c) * LANES, LANES), LANES)
                out[c, start : start + many] = first[rows, lanes].reshape(many, BS, LANES)


def token_kernel(order, at, *refs):
    count = len(order)
    mine, theirs, gain, weights = refs[:count], *refs[count : count + 3]
    outs, (first, ready, total, held, done) = refs[count + 3 : -5], refs[-5:]
    core = at[1]
    trip = theirs.shape[1]
    groups = len(outs)
    steps = held.shape[0]
    pair = weights.shape[2]
    copies = [
        pltpu.make_async_copy(weights.at[:, i // pair, i % pair], held.at[i], done.at[i])
        for i in range(steps)
    ]
    for copy in copies:
        copy.start()
    for i, ref in enumerate(mine):
        place = lax.rem(at[0] - order[i] + count, count)
        row = (lax.rem(place, groups) * (count // groups) + place // groups) * BS
        rows = pl.ds(pl.multiple_of(row, BS), BS)
        for t in range(trip):
            own = pl.ds(pl.multiple_of((core * trip + t) * LANES, LANES), LANES)
            first[rows, own] = ref[core, t]
            other = pl.ds(pl.multiple_of(((1 - core) * trip + t) * LANES, LANES), LANES)
            first[rows, other] = theirs[i, t]
    for r in range(2 * trip):
        lanes = slice(r * LANES, (r + 1) * LANES)
        values = first[:, lanes].astype(F32)
        total[:, lanes] = values
        values = values - jnp.mean(values, axis=0, keepdims=True)
        spread = jnp.mean(values * values, axis=0, keepdims=True)
        ready[:, lanes] = (values * lax.rsqrt(spread + EPSILON) * gain[...]).astype(BF16)
    side = first.shape[0]
    for i, copy in enumerate(copies):
        copy.wait()
        hidden = dot(held[i, :, 0].reshape(-1, side), ready[...])
        hidden = jax.nn.gelu(hidden).astype(BF16)
        total[...] += dot(held[i, :, 1].reshape(side, -1), hidden)
    chans = outs[0].shape[1]
    for d, out in enumerate(outs):
        low = lax.rem(lax.rem(at[0], groups) + d, groups)
        rows = pl.ds(pl.multiple_of(low * chans, chans), chans)
        for r in range(out.shape[0]):
            out[r] = total[rows, r * LANES : (r + 1) * LANES].astype(BF16)


def on_device(tokens, gain_first, mode_first, mode_second, kept_lat, gain_second, w_up, w_down):
    rows, chans, cols = tokens.shape
    lat_n, zh_n, co_n, ch_n = (lax.axis_size(a) for a in ("lat", "zh", "co", "ch"))
    lon_n, z_n = zh_n * co_n, zh_n * ch_n
    width = cols * lon_n
    height = rows * lat_n
    full = chans * ch_n
    dests = lat_n * co_n
    half = rows // co_n
    trip = half // ch_n
    lat, zh, co, ch = (lax.axis_index(a) for a in ("lat", "zh", "co", "ch"))
    lon = zh * co_n + co
    z = zh * ch_n + ch
    swap = [(0, 1), (1, 0)]

    def ring(array, axes, count, step):
        return lax.ppermute(array, axes, [(i, (i + step) % count) for i in range(count)])

    piece_n = w_up.shape[1] // lat_n
    piece = jnp.stack(
        [
            lax.dynamic_slice_in_dim(w, lat * piece_n, piece_n, axis=1).T
            for w in (w_up, w_down)
        ]
    )
    pieces = [
        lax.ppermute(
            piece,
            ("co", "ch"),
            [(c * ch_n + i, c * ch_n + (i + 2 * c + d) % ch_n) for c in range(co_n) for i in range(ch_n)],
        )
        for d in range(ch_n // co_n)
    ]
    pieces = jnp.stack(pieces)

    values = tokens.astype(F32)
    sums = jnp.stack([jnp.sum(values, axis=1), jnp.sum(values * values, axis=1)])
    sums = sums + sum(ring(sums, "ch", ch_n, d) for d in range(1, ch_n))

    block_gain = lax.dynamic_slice_in_dim(gain_first, zh * BS, BS)
    block_gain = jnp.broadcast_to(block_gain[:, None], (BS, cols))
    second_gain = jnp.broadcast_to(gain_second[:, None], (full, cols))
    place = jnp.stack([co, zh, lon]).astype(jnp.int32)
    column = jnp.stack([z, co]).astype(jnp.int32)
    pieces, sums, sent, block_gain, second_gain, place, column = lax.optimization_barrier(
        (pieces, sums, tokens, block_gain, second_gain, place, column)
    )
    weights = lax.all_gather(pieces, ("lat", "co"))
    own = sent.reshape(ch_n, co_n, trip, zh_n, BS, cols)
    chunks = ((0, 1), (1, trip - 1))
    sizes = [ch_n * count * BS for _, count in chunks]

    def to_far(array, chunk):
        array = lax.slice_in_dim(array, chunk[0], chunk[0] + chunk[1], axis=2)
        return lax.ppermute(
            lax.dynamic_index_in_dim(array, 1 - zh, axis=3, keepdims=False), "zh", swap
        )

    def to_near(array):
        return lax.ppermute(
            lax.dynamic_index_in_dim(array, 1 - co, axis=1, keepdims=False), "co", swap
        )

    far = to_far(own, chunks[0])
    chip_sums = jnp.stack([sums, lax.ppermute(sums, "co", swap)])
    partner_sums = lax.ppermute(chip_sums, "zh", swap)
    order = np.arange(height).reshape(lat_n, ch_n, co_n, trip).transpose(1, 3, 0, 2)
    order = np.concatenate([order[:, a : a + n].reshape(-1) for a, n in chunks])
    left = lat_table(kept_lat, height, order)
    kept = kept_lat.shape[0]
    first_w = mode_weight(lax.dynamic_index_in_dim(mode_first, zh, axis=0, keepdims=False))
    second_w = mode_weight(lax.dynamic_index_in_dim(mode_second, zh, axis=0, keepdims=False))
    (far, chip_sums, partner_sums, own), tables = lax.optimization_barrier(
        ((far, chip_sums, partner_sums, own), (left, first_w, second_w))
    )
    left, first_w, second_w = tables
    fars = [far, to_far(own, chunks[1])]

    forward, inverse = lon_tables(width, dests)
    forward = jnp.asarray(forward, BF16)
    wide_n = half * BS
    columns, bases = [], []
    for chunk, size, far in zip(chunks, sizes, fars):
        near = lax.slice_in_dim(own, chunk[0], chunk[0] + chunk[1], axis=2)
        near = to_near(lax.dynamic_index_in_dim(near, zh, axis=3, keepdims=False))
        spec, base = call(
            functools.partial(forward_kernel, float(full), chunk[0]),
            place,
            (own, near, far, to_near(far), chip_sums, partner_sums, block_gain, forward),
            (
                jax.ShapeDtypeStruct((dests, 2 * KW // dests, size), BF16),
                jax.ShapeDtypeStruct((size, width), F32),
            ),
            [
                pltpu.VMEM((size, width), BF16),
                pltpu.VMEM((lon_n, rows, cols), F32),
                pltpu.VMEM((lon_n, rows, cols), F32),
            ],
            4 * KW * width * size,
        )
        columns.append(
            lax.all_to_all(spec, ("lat", "co"), split_axis=0, concat_axis=0, tiled=True)
        )
        bases.append(base)

    modes = KW // dests
    (back,) = call(
        functools.partial(middle_kernel, len(columns)),
        place,
        (*columns, left, first_w, second_w),
        (jax.ShapeDtypeStruct((dests, 2 * modes, wide_n), BF16),),
        [
            pltpu.VMEM((wide_n // LANES, dests * 2 * modes, LANES), F32),
            pltpu.VMEM((2 * height, modes * LANES), BF16),
            pltpu.VMEM((2 * kept, modes * LANES), BF16),
        ],
        16 * height * kept * modes * LANES,
    )
    returned = lax.all_to_all(back, ("lat", "co"), split_axis=0, concat_axis=0, tiled=True)

    returned, weights = lax.optimization_barrier((returned, weights))
    weights = weights.reshape(lat_n, co_n, ch_n // co_n, 2, piece_n, full)
    firsts = call(
        functools.partial(inverse_kernel, chunks),
        column,
        (returned.reshape(2 * KW, wide_n), jnp.asarray(inverse, BF16), *bases),
        tuple(jax.ShapeDtypeStruct((co_n, trip, BS, cols), BF16) for _ in range(z_n)),
        [pltpu.VMEM((wide_n, width), BF16)],
        4 * KW * width * wide_n,
        SMALL,
    )
    order = sorted(range(z_n), key=lambda d: (min(d, z_n - d), -d))
    mine = [ring(firsts[d], ("zh", "ch"), z_n, d) if d else firsts[0] for d in order]
    theirs = jnp.stack(
        [lax.dynamic_index_in_dim(m, 1 - co, axis=0, keepdims=False) for m in mine]
    )
    theirs = lax.ppermute(theirs, "co", swap)

    tokens_n = co_n * trip * cols
    once = [*mine, theirs, second_gain]
    results = pl.pallas_call(
        functools.partial(token_kernel, order),
        grid_spec=pltpu.PrefetchScalarGridSpec(
            num_scalar_prefetch=1,
            grid=(1,),
            in_specs=[whole(a.shape) for a in once] + [pl.BlockSpec(memory_space=pltpu.HBM)],
            out_specs=[whole((co_n * trip, chans, cols))] * ch_n,
            scratch_shapes=[
                pltpu.VMEM((full, tokens_n), BF16),
                pltpu.VMEM((full, tokens_n), BF16),
                pltpu.VMEM((full, tokens_n), F32),
                pltpu.VMEM((ch_n, lat_n, 2, piece_n, full), BF16),
                pltpu.SemaphoreType.DMA((ch_n,)),
            ],
        ),
        out_shape=[jax.ShapeDtypeStruct((co_n * trip, chans, cols), BF16)] * ch_n,
        compiler_params=pltpu.CompilerParams(vmem_limit_bytes=LARGE),
        cost_estimate=pl.CostEstimate(
            flops=4 * full * full * ch_n * tokens_n,
            bytes_accessed=weights.size * 2,
            transcendentals=full * ch_n * tokens_n,
        ),
    )(column, *once, weights)
    output = jnp.zeros((ch_n, co_n * trip, chans, cols), BF16)
    for d, piece in enumerate(results):
        piece = piece if d == 0 else ring(piece, "ch", ch_n, d)
        output = lax.dynamic_update_index_in_dim(output, piece, lax.rem(ch - d + ch_n, ch_n), 0)
    return output.reshape(rows, chans, cols)


def solution(mesh):
    grid = mesh.devices
    lat_n, lon_n, ch_n = grid.shape
    split = Mesh(grid.reshape(lat_n, 2, lon_n // 2, ch_n), ("lat", "zh", "co", "ch"))
    lon = ("zh", "co")
    return jax.shard_map(
        on_device,
        mesh=split,
        in_specs=(
            P("lat", "ch", lon),
            P("ch"),
            P("ch", None),
            P("ch", None),
            P(),
            P(),
            P(None, "ch"),
            P("ch", None),
        ),
        out_specs=P("lat", "ch", lon),
        check_vma=False,
    )
```

```python
import functools
import math

import jax
import jax.numpy as jnp
import numpy as np
from jax import lax
from jax.experimental import pallas as pl
from jax.experimental.pallas import tpu as pltpu
from jax.sharding import Mesh, PartitionSpec as P

BS = 96
KW = 256
LANES = 128
SHRINK = 0.01
EPSILON = 1e-05
BF16 = jnp.bfloat16
F32 = jnp.float32
SMALL = 32 * 1024 * 1024
LARGE = 56 * 1024 * 1024


def dot(left, right, dims=((1,), (0,))):
    return lax.dot_general(left, right, (dims, ((), ())), preferred_element_type=F32)


def whole(shape):
    return pl.BlockSpec(shape, lambda *_: (0,) * len(shape))


def call(kernel, scalars, args, outs, scratch, flops, limit=SMALL):
    moved = sum(a.size * a.dtype.itemsize for a in (*args, *outs))
    return pl.pallas_call(
        kernel,
        grid_spec=pltpu.PrefetchScalarGridSpec(
            num_scalar_prefetch=1,
            grid=(1,),
            in_specs=[whole(a.shape) for a in args],
            out_specs=[whole(o.shape) for o in outs],
            scratch_shapes=scratch,
        ),
        out_shape=outs,
        compiler_params=pltpu.CompilerParams(vmem_limit_bytes=limit),
        cost_estimate=pl.CostEstimate(flops=flops, bytes_accessed=moved, transcendentals=0),
    )(scalars, *args)


def lon_tables(width, dests):
    k = np.arange(KW)
    angle = 2.0 * np.pi * (k[:, None] * np.arange(width)[None, :] % width) / width
    both = np.stack([np.cos(angle), -np.sin(angle)]) / math.sqrt(width)
    forward = both.reshape(2, dests, KW // dests, width).transpose(1, 0, 2, 3)
    weights = np.where(k == 0, 1.0, 2.0)
    inverse = (both * weights[None, :, None]).reshape(2, dests, KW // dests, width)
    inverse = inverse.transpose(1, 0, 2, 3)
    return forward.reshape(2 * KW, width), inverse.reshape(2 * KW, width)


def lat_table(kept_lat, height, order):
    h = np.arange(height)
    angle = 2.0 * np.pi * (h[:, None] * h[order][None, :] % height) / height
    cosine, sine = np.cos(angle) / math.sqrt(height), np.sin(angle) / math.sqrt(height)
    table = np.concatenate([cosine, sine, -sine, cosine], axis=1)
    pick = (kept_lat[:, None] == jnp.arange(height)[None, :]).astype(BF16)
    kept = dot(pick, jnp.asarray(table, BF16)).astype(BF16)
    return jnp.concatenate([kept[:, : 2 * height], kept[:, 2 * height :]], axis=0)


def mode_weight(flat):
    weight = flat.reshape(2, BS, BS)
    weight = jnp.pad(weight, ((0, 0), (0, LANES - BS), (0, LANES - BS)))
    return jnp.concatenate(
        [
            jnp.concatenate([weight[0], weight[1]], axis=1),
            jnp.concatenate([-weight[1], weight[0]], axis=1),
        ],
        axis=0,
    ).astype(BF16)


def forward_kernel(full, start, at, own, near, far, across, chip, partner, gain, table, *refs):
    spec, base, normed, mean, scale = refs
    for d in range(4):
        stats = (chip if d < 2 else partner)[d % 2] / full
        mean[d] = stats[0]
        scale[d] = lax.rsqrt(stats[1] - stats[0] * stats[0] + EPSILON)
    core, high, lon = at[0], at[1], at[2]
    trip, count = own.shape[2], near.shape[1]
    parts = (
        lambda c, t: own[c, core, start + t, high],
        lambda c, t: near[c, t],
        lambda c, t: far[c, core, t],
        lambda c, t: across[c, t],
    )
    for d, part in enumerate(parts):
        lanes = pl.ds(pl.multiple_of((lon ^ d) * LANES, LANES), LANES)
        for c in range(near.shape[0]):
            for t in range(count):
                low = 2 * c * trip + start + t
                picked = []
                for ref in (mean, scale):
                    rows = ref[d, low : low + 1], ref[d, low + trip : low + trip + 1]
                    picked.append(jnp.where(core == 0, *rows))
                values = part(c, t).astype(F32)
                value = ((values - picked[0]) * picked[1] * gain[...]).astype(BF16)
                rows = slice((c * count + t) * BS, (c * count + t + 1) * BS)
                normed[rows, lanes] = value
                base[rows, lanes] = values + value.astype(F32)
    result = dot(table[...], normed[...], ((1,), (1,)))
    spec[...] = result.astype(BF16).reshape(spec.shape)


def middle_kernel(parts, at, *refs):
    columns, (left, first_w, second_w) = refs[:parts], refs[parts : parts + 3]
    out, wide, stacked, mid = refs[parts + 3 :]
    srcs, pairs, inner = out.shape
    modes = pairs // 2
    local = inner // BS
    height = srcs * local
    kept = left.shape[0] // 2
    tiles = inner // LANES
    j = 0
    for column in columns:
        for k in range(column.shape[2] // LANES):
            part = column[:, :, k * LANES : (k + 1) * LANES]
            wide[j] = part.reshape(srcs * pairs, LANES).astype(F32)
            j += 1
    blank = jnp.zeros((srcs, LANES), F32)
    for t in range(2):
        for k in range(modes):
            take = pl.ds(t * modes + k, srcs, stride=pairs)
            one = jnp.concatenate([wide[j, take, :] for j in range(tiles)] + [blank], axis=1)
            for r in range(local):
                rows = slice(t * height + r * srcs, t * height + (r + 1) * srcs)
                stacked[rows, k * LANES : (k + 1) * LANES] = one[
                    :, r * BS : r * BS + LANES
                ].astype(BF16)
    moved = dot(left[...], stacked[...]).astype(BF16)
    for k in range(modes):
        lanes = slice(k * LANES, (k + 1) * LANES)
        both = jnp.concatenate([moved[:kept, lanes], moved[kept:, lanes]], axis=1)
        both = jnp.maximum(dot(both, first_w[...]), 0.0).astype(BF16)
        both = dot(both, second_w[...])
        both = jnp.where(
            both > SHRINK, both - SHRINK, jnp.where(both < -SHRINK, both + SHRINK, 0.0)
        ).astype(BF16)
        mid[:kept, lanes] = both[:, :LANES]
        mid[kept:, lanes] = both[:, LANES:]
    back = dot(left[...], mid[...], ((0,), (0,)))
    for t in range(2):
        for k in range(modes):
            lanes = slice(k * LANES, k * LANES + BS)
            one = jnp.concatenate(
                [
                    back[t * height + r * srcs : t * height + (r + 1) * srcs, lanes]
                    for r in range(local)
                ],
                axis=1,
            )
            for j in range(tiles):
                put = pl.ds(t * modes + k, srcs, stride=pairs)
                wide[j, put, :] = one[:, j * LANES : (j + 1) * LANES]
    for j in range(tiles):
        part = wide[j].astype(BF16).reshape(srcs, pairs, LANES)
        out[:, :, j * LANES : (j + 1) * LANES] = part


def inverse_kernel(chunks, at, returned, table, *refs):
    bases, outs, first = refs[: len(chunks)], refs[len(chunks) : -1], refs[-1]
    field = dot(returned[...], table[...], ((0,), (0,))).astype(BF16).astype(F32)
    ahead = 0
    for base in bases:
        size = base.shape[0]
        first[ahead : ahead + size] = (base[...] + field[ahead : ahead + size]).astype(BF16)
        ahead += size
    count = len(outs)
    cores, trip = outs[0].shape[0], outs[0].shape[1]
    groups = first.shape[0] // (trip * BS)
    for d, out in enumerate(outs):
        place = lax.rem(at[0] + d, count)
        high, low = place // groups, lax.rem(place, groups)
        for start, many in chunks:
            row = start * groups * BS + low * (many * BS)
            rows = pl.ds(pl.multiple_of(row, BS), many * BS)
            for c in range(cores):
                lanes = pl.ds(pl.multiple_of((high * cores + c) * LANES, LANES), LANES)
                out[c, start : start + many] = first[rows, lanes].reshape(many, BS, LANES)


def token_kernel(order, at, *refs):
    count = len(order)
    mine, theirs, gain, weights = refs[:count], *refs[count : count + 3]
    outs, (first, ready, total, held, done) = refs[count + 3 : -5], refs[-5:]
    core = at[1]
    trip = theirs.shape[1]
    groups = len(outs)
    steps = held.shape[0]
    pair = weights.shape[2]
    copies = [
        pltpu.make_async_copy(weights.at[:, i // pair, i % pair], held.at[i], done.at[i])
        for i in range(steps)
    ]
    for copy in copies:
        copy.start()
    for i, ref in enumerate(mine):
        place = lax.rem(at[0] - order[i] + count, count)
        row = (lax.rem(place, groups) * (count // groups) + place // groups) * BS
        rows = pl.ds(pl.multiple_of(row, BS), BS)
        for t in range(trip):
            own = pl.ds(pl.multiple_of((core * trip + t) * LANES, LANES), LANES)
            first[rows, own] = ref[core, t]
            other = pl.ds(pl.multiple_of(((1 - core) * trip + t) * LANES, LANES), LANES)
            first[rows, other] = theirs[i, t]
    for r in range(2 * trip):
        lanes = slice(r * LANES, (r + 1) * LANES)
        values = first[:, lanes].astype(F32)
        total[:, lanes] = values
        values = values - jnp.mean(values, axis=0, keepdims=True)
        spread = jnp.mean(values * values, axis=0, keepdims=True)
        ready[:, lanes] = (values * lax.rsqrt(spread + EPSILON) * gain[...]).astype(BF16)
    side = first.shape[0]
    for i, copy in enumerate(copies):
        copy.wait()
        hidden = dot(held[i, :, 0].reshape(-1, side), ready[...])
        hidden = jax.nn.gelu(hidden).astype(BF16)
        total[...] += dot(held[i, :, 1].reshape(side, -1), hidden)
    chans = outs[0].shape[1]
    for d, out in enumerate(outs):
        low = lax.rem(lax.rem(at[0], groups) + d, groups)
        rows = pl.ds(pl.multiple_of(low * chans, chans), chans)
        for r in range(out.shape[0]):
            out[r] = total[rows, r * LANES : (r + 1) * LANES].astype(BF16)


def on_device(tokens, gain_first, mode_first, mode_second, kept_lat, gain_second, w_up, w_down):
    rows, chans, cols = tokens.shape
    lat_n, zh_n, co_n, ch_n = (lax.axis_size(a) for a in ("lat", "zh", "co", "ch"))
    lon_n, z_n = zh_n * co_n, zh_n * ch_n
    width = cols * lon_n
    height = rows * lat_n
    full = chans * ch_n
    dests = lat_n * co_n
    half = rows // co_n
    trip = half // ch_n
    lat, zh, co, ch = (lax.axis_index(a) for a in ("lat", "zh", "co", "ch"))
    lon = zh * co_n + co
    z = zh * ch_n + ch
    swap = [(0, 1), (1, 0)]

    def ring(array, axes, count, step):
        return lax.ppermute(array, axes, [(i, (i + step) % count) for i in range(count)])

    piece_n = w_up.shape[1] // lat_n
    piece = jnp.stack(
        [
            lax.dynamic_slice_in_dim(w, lat * piece_n, piece_n, axis=1).T
            for w in (w_up, w_down)
        ]
    )
    pieces = [
        lax.ppermute(
            piece,
            ("co", "ch"),
            [(c * ch_n + i, c * ch_n + (i + 2 * c + d) % ch_n) for c in range(co_n) for i in range(ch_n)],
        )
        for d in range(ch_n // co_n)
    ]
    pieces = jnp.stack(pieces)

    values = tokens.astype(F32)
    sums = jnp.stack([jnp.sum(values, axis=1), jnp.sum(values * values, axis=1)])
    sums = sums + sum(ring(sums, "ch", ch_n, d) for d in range(1, ch_n))

    block_gain = lax.dynamic_slice_in_dim(gain_first, zh * BS, BS)
    block_gain = jnp.broadcast_to(block_gain[:, None], (BS, cols))
    second_gain = jnp.broadcast_to(gain_second[:, None], (full, cols))
    place = jnp.stack([co, zh, lon]).astype(jnp.int32)
    column = jnp.stack([z, co]).astype(jnp.int32)
    pieces, sums, sent, block_gain, second_gain, place, column = lax.optimization_barrier(
        (pieces, sums, tokens, block_gain, second_gain, place, column)
    )
    weights = lax.all_gather(pieces, ("lat", "co"))
    own = sent.reshape(ch_n, co_n, trip, zh_n, BS, cols)
    chunks = ((0, 1), (1, trip - 1))
    sizes = [ch_n * count * BS for _, count in chunks]

    def to_far(array, chunk):
        array = lax.slice_in_dim(array, chunk[0], chunk[0] + chunk[1], axis=2)
        return lax.ppermute(
            lax.dynamic_index_in_dim(array, 1 - zh, axis=3, keepdims=False), "zh", swap
        )

    def to_near(array):
        return lax.ppermute(
            lax.dynamic_index_in_dim(array, 1 - co, axis=1, keepdims=False), "co", swap
        )

    far = to_far(own, chunks[0])
    chip_sums = jnp.stack([sums, lax.ppermute(sums, "co", swap)])
    partner_sums = lax.ppermute(chip_sums, "zh", swap)
    order = np.arange(height).reshape(lat_n, ch_n, co_n, trip).transpose(1, 3, 0, 2)
    order = np.concatenate([order[:, a : a + n].reshape(-1) for a, n in chunks])
    left = lat_table(kept_lat, height, order)
    kept = kept_lat.shape[0]
    first_w = mode_weight(lax.dynamic_index_in_dim(mode_first, zh, axis=0, keepdims=False))
    second_w = mode_weight(lax.dynamic_index_in_dim(mode_second, zh, axis=0, keepdims=False))
    (far, chip_sums, partner_sums, own), tables = lax.optimization_barrier(
        ((far, chip_sums, partner_sums, own), (left, first_w, second_w))
    )
    left, first_w, second_w = tables
    fars = [far, to_far(own, chunks[1])]

    forward, inverse = lon_tables(width, dests)
    forward = jnp.asarray(forward, BF16)
    wide_n = half * BS
    columns, bases = [], []
    for chunk, size, far in zip(chunks, sizes, fars):
        near = lax.slice_in_dim(own, chunk[0], chunk[0] + chunk[1], axis=2)
        near = to_near(lax.dynamic_index_in_dim(near, zh, axis=3, keepdims=False))
        spec, base = call(
            functools.partial(forward_kernel, float(full), chunk[0]),
            place,
            (own, near, far, to_near(far), chip_sums, partner_sums, block_gain, forward),
            (
                jax.ShapeDtypeStruct((dests, 2 * KW // dests, size), BF16),
                jax.ShapeDtypeStruct((size, width), F32),
            ),
            [
                pltpu.VMEM((size, width), BF16),
                pltpu.VMEM((lon_n, rows, cols), F32),
                pltpu.VMEM((lon_n, rows, cols), F32),
            ],
            4 * KW * width * size,
            LARGE,
        )
        columns.append(
            lax.all_to_all(spec, ("lat", "co"), split_axis=0, concat_axis=0, tiled=True)
        )
        bases.append(base)

    modes = KW // dests
    (back,) = call(
        functools.partial(middle_kernel, len(columns)),
        place,
        (*columns, left, first_w, second_w),
        (jax.ShapeDtypeStruct((dests, 2 * modes, wide_n), BF16),),
        [
            pltpu.VMEM((wide_n // LANES, dests * 2 * modes, LANES), F32),
            pltpu.VMEM((2 * height, modes * LANES), BF16),
            pltpu.VMEM((2 * kept, modes * LANES), BF16),
        ],
        16 * height * kept * modes * LANES,
    )
    returned = lax.all_to_all(back, ("lat", "co"), split_axis=0, concat_axis=0, tiled=True)

    returned, weights = lax.optimization_barrier((returned, weights))
    weights = weights.reshape(lat_n, co_n, ch_n // co_n, 2, piece_n, full)
    firsts = call(
        functools.partial(inverse_kernel, chunks),
        column,
        (returned.reshape(2 * KW, wide_n), jnp.asarray(inverse, BF16), *bases),
        tuple(jax.ShapeDtypeStruct((co_n, trip, BS, cols), BF16) for _ in range(z_n)),
        [pltpu.VMEM((wide_n, width), BF16)],
        4 * KW * width * wide_n,
        SMALL,
    )
    order = sorted(range(z_n), key=lambda d: (min(d, z_n - d), -d))
    mine = [ring(firsts[d], ("zh", "ch"), z_n, d) if d else firsts[0] for d in order]
    theirs = jnp.stack(
        [lax.dynamic_index_in_dim(m, 1 - co, axis=0, keepdims=False) for m in mine]
    )
    theirs = lax.ppermute(theirs, "co", swap)

    tokens_n = co_n * trip * cols
    once = [*mine, theirs, second_gain]
    results = pl.pallas_call(
        functools.partial(token_kernel, order),
        grid_spec=pltpu.PrefetchScalarGridSpec(
            num_scalar_prefetch=1,
            grid=(1,),
            in_specs=[whole(a.shape) for a in once] + [pl.BlockSpec(memory_space=pltpu.HBM)],
            out_specs=[whole((co_n * trip, chans, cols))] * ch_n,
            scratch_shapes=[
                pltpu.VMEM((full, tokens_n), BF16),
                pltpu.VMEM((full, tokens_n), BF16),
                pltpu.VMEM((full, tokens_n), F32),
                pltpu.VMEM((ch_n, lat_n, 2, piece_n, full), BF16),
                pltpu.SemaphoreType.DMA((ch_n,)),
            ],
        ),
        out_shape=[jax.ShapeDtypeStruct((co_n * trip, chans, cols), BF16)] * ch_n,
        compiler_params=pltpu.CompilerParams(vmem_limit_bytes=LARGE),
        cost_estimate=pl.CostEstimate(
            flops=4 * full * full * ch_n * tokens_n,
            bytes_accessed=weights.size * 2,
            transcendentals=full * ch_n * tokens_n,
        ),
    )(column, *once, weights)
    output = jnp.zeros((ch_n, co_n * trip, chans, cols), BF16)
    for d, piece in enumerate(results):
        piece = piece if d == 0 else ring(piece, "ch", ch_n, d)
        output = lax.dynamic_update_index_in_dim(output, piece, lax.rem(ch - d + ch_n, ch_n), 0)
    return output.reshape(rows, chans, cols)


def solution(mesh):
    grid = mesh.devices
    lat_n, lon_n, ch_n = grid.shape
    split = Mesh(grid.reshape(lat_n, 2, lon_n // 2, ch_n), ("lat", "zh", "co", "ch"))
    lon = ("zh", "co")
    return jax.shard_map(
        on_device,
        mesh=split,
        in_specs=(
            P("lat", "ch", lon),
            P("ch"),
            P("ch", None),
            P("ch", None),
            P(),
            P(),
            P(None, "ch"),
            P("ch", None),
        ),
        out_specs=P("lat", "ch", lon),
        check_vma=False,
    )
```
